128 devices in a mesh: req: 4 (over y), mp: 32 (over z, x, core).
Axes of the slice: x: 4, y: 4, z: 4, core: 2. Of those that a mesh axis runs over, the one named last changes fastest.
Arguments:
- tokens: bfloat16 [1024, 2048], P('req'), may hold values from -6 to 6
- lengths: int32 [4, 8], P('req'), may hold values from 1 to 80, 256 in all within a row
- response: int32 [1024], P('req'), may hold values 0 or 1
- targets: int32 [1024], replicated, may hold values from 0 to 128255, as said below
- attn_gain: float32 [2, 2048], replicated, may hold values from 0.5 to 1.5
- w_query: bfloat16 [2, 2048, 2048], P(None, None, 'mp')
- w_key: bfloat16 [2, 2048, 512], replicated, may hold values from -0.125 to 0.125
- w_value: bfloat16 [2, 2048, 512], replicated, may hold values from -0.125 to 0.125
- output_weight: bfloat16 [2, 2048, 2048], P(None, 'mp'), may hold values from -0.125 to 0.125
- mlp_gain: float32 [2, 2048], replicated, may hold values from 0.5 to 1.5
- w_gate: bfloat16 [2, 2048, 8192], P(None, None, 'mp'), may hold values from -0.125 to 0.125
- w_up: bfloat16 [2, 2048, 8192], P(None, None, 'mp'), may hold values from -0.125 to 0.125
- w_down: bfloat16 [2, 8192, 2048], P(None, 'mp'), may hold values from -0.0625 to 0.0625
- final_gain: float32 [2, 2048], replicated, may hold values from 0.5 to 1.5
- w_head: bfloat16 [2, 2048, 128256], P(None, None, ('req', 'mp'))
Outputs:
- token_diff: float32 [1024], P(('req', 'mp'))
- request_sum: float32 [4, 8], P('req')
- request_peak: float32 [4, 8], P('req')
The draws below stay inside these ranges and needn't reach their ends.
Inputs may be any that keep to these rules, and one draw needn't show every extreme that they name: `lengths`: each row sums to 256; some request of each tenant has exactly 80 tokens. `targets`: vocabulary ids.
All inputs are finite; a program needn't handle non-finite values. No bound on the sum of `response` on one device may be relied on, other than what follows from the above.
Results may differ from the reference program's by a relative error of at most 0.04.
Values may be sent and summed in bfloat16 or wider, within the bound.
A program may use at most 128 MiB of HBM per device.

```python
import math
import jax
import jax.numpy as jnp
import numpy as np
from jax import lax

D = 2048
HEADS = 32
KV_HEADS = 8
HEAD_DIM = 64
FF = 8192
V_DEV = 1002
TOK_GRP = 256
RPT = 8
TENANTS = 4
TOKENS = 1024
V = 128256
MOST_LEN = 80
DEVICES = 128


def draw_targets(key, part):
    per_block = TOKENS // DEVICES
    row_ids = jnp.arange(TOKENS, dtype=jnp.int32)
    block_ids = row_ids // per_block
    inner_ids = row_ids % per_block
    mixed_ids = inner_ids + block_ids
    structured = mixed_ids % 2 == 0
    partner_table = jnp.array([1, DEVICES - 1, DEVICES // 2], dtype=jnp.int32)
    partner = partner_table[mixed_ids // 2 % 3]
    slice_fixed = (block_ids + partner) % DEVICES
    slice_random = jax.random.randint(jax.random.fold_in(key, 3), (TOKENS,), 0, DEVICES, dtype=jnp.int32)
    column = jax.random.randint(jax.random.fold_in(key, 5), (TOKENS,), 0, V_DEV, dtype=jnp.int32)
    chosen_slice = jnp.where(structured, slice_fixed, slice_random)
    picked = (chosen_slice * V_DEV + column).astype(jnp.int32)
    picked = jnp.where(row_ids == 0, jnp.int32(0), picked)
    picked = jnp.where(row_ids == TOKENS - 1, jnp.int32(V - 1), picked)
    return picked.astype(jnp.int32)


def draw_w_query(key, part):
    base_values = jax.random.normal(key, (2, D, HEADS * HEAD_DIM), jnp.float32)
    base_values = jnp.clip(base_values, -6.0, 6.0) / jnp.sqrt(jnp.float32(D))
    return base_values.astype(jnp.bfloat16)


def draw_w_head(key, part):
    base_values = jax.random.normal(key, (2, D, V), jnp.float32)
    base_values = jnp.clip(base_values, -6.0, 6.0) * (3.0 / jnp.sqrt(jnp.float32(D)))
    return base_values.astype(jnp.bfloat16)


def place_ends(values, rng, least, largest):
    longest = values.shape.index(max(values.shape))
    spots = []
    for shift in (0, 1):
        where = [jax.random.randint(jax.random.fold_in(rng, axis), (), 0, length) for axis, length in enumerate(values.shape)]
        where[longest] = (where[longest] + shift) % values.shape[longest]
        spots.append(tuple(where))
    return values.at[spots[0]].set(least).at[spots[1]].set(largest)


def steps_of(rng, shape, cuts, least, high):
    gain, own = 1.0, jax.random.fold_in(rng, 6)
    for dim, shards_of in cuts:
        draws = jnp.exp(jax.random.uniform(jax.random.fold_in(own, dim), (shards_of,), jnp.float32, least / len(cuts), high / len(cuts)))
        gain = gain * jnp.repeat(draws, shape[dim] // shards_of).reshape([-1 if axis == dim else 1 for axis in range(len(shape))])
    return gain


def profile(amount, total, most, slope):
    weights = [(1 << 20) // math.isqrt(rank ** slope) + 1 for rank in range(2, amount + 1)]
    spare, holding = total - most - (amount - 1), [1] * (amount - 1)
    while spare > 0:
        candidates = [i for i in range(amount - 1) if holding[i] < most]
        pool, left = sum([weights[i] for i in candidates]), spare
        for i in candidates:
            addition = min(most - holding[i], max(1, left * weights[i] // pool), spare)
            holding[i] = holding[i] + addition
            spare = spare - addition
    return np.array([most] + holding)


def ragged(stream_key, number_of, total, bound, lean):
    if number_of == 2:
        one = jax.random.randint(stream_key, (), max(1, total - bound), min(bound, total - 1) + 1)
        return jnp.stack([one, total - one])
    sizes = jnp.asarray(profile(number_of, total, bound, lean), jnp.int32)
    twos = (number_of - 1) // 2
    donor, receiver = sizes[1:1 + 2 * twos:2], sizes[2:2 + 2 * twos:2]
    room = jnp.minimum(donor - 1, bound - receiver)
    passed = jax.random.randint(jax.random.fold_in(stream_key, 1), (twos,), 0, 1 << 20) % (room + 1)
    sizes = sizes.at[1:1 + 2 * twos:2].set(donor - passed).at[2:2 + 2 * twos:2].set(receiver + passed)
    return sizes[jax.random.permutation(jax.random.fold_in(stream_key, 2), number_of)]


def normal_values(own_key, dims, deviation, most, split=(), kind=jnp.bfloat16):
    values = deviation * jax.random.normal(own_key, dims, jnp.float32)
    if split:
        values = values * steps_of(own_key, dims, split, -0.22, 0.18)
    return jnp.clip(values, -most, most).astype(kind)


def setup_inputs(seed: int = 0) -> dict:
    streams_of = jax.random.split(jax.random.key(seed), 16)
    tokens = normal_values(streams_of[0], (TOKENS, D), 1.0, 6.0, ((0, 4),))
    lengths = jax.vmap(lambda own: ragged(own, RPT, TOK_GRP, MOST_LEN, 2))(jax.random.split(streams_of[1], TENANTS)).reshape((TENANTS, RPT)).astype(jnp.int32)
    response = place_ends((jax.random.randint(streams_of[2], (TOKENS,), 0, 8) < 3).astype(jnp.int32), jax.random.fold_in(streams_of[2], 1), 0, 1)
    targets = draw_targets(jax.random.fold_in(streams_of[15], 71), 0)
    attn_gain = jnp.clip(1.0 + 0.1 * jax.random.normal(streams_of[4], (2, D), jnp.float32), 0.5, 1.5)
    w_query = draw_w_query(jax.random.fold_in(streams_of[15], 71), 0)
    w_key = normal_values(streams_of[6], (2, D, KV_HEADS * HEAD_DIM), D ** -0.5, 0.125)
    w_value = normal_values(streams_of[7], (2, D, KV_HEADS * HEAD_DIM), D ** -0.5, 0.125)
    output_weight = normal_values(streams_of[8], (2, HEADS * HEAD_DIM, D), (HEADS * HEAD_DIM) ** -0.5, 0.125, ((1, 32),))
    mlp_gain = jnp.clip(1.0 + 0.1 * jax.random.normal(streams_of[9], (2, D), jnp.float32), 0.5, 1.5)
    w_gate = normal_values(streams_of[10], (2, D, FF), D ** -0.5, 0.125, ((2, 32),))
    w_up = normal_values(streams_of[11], (2, D, FF), D ** -0.5, 0.125, ((2, 32),))
    w_down = normal_values(streams_of[12], (2, FF, D), FF ** -0.5, 0.0625, ((1, 32),))
    final_gain = jnp.clip(1.0 + 0.1 * jax.random.normal(streams_of[13], (2, D), jnp.float32), 0.5, 1.5)
    w_head = draw_w_head(jax.random.fold_in(streams_of[15], 71), 0)
    return dict(tokens=tokens, lengths=lengths, response=response, targets=targets, attn_gain=attn_gain, w_query=w_query, w_key=w_key, w_value=w_value, output_weight=output_weight, mlp_gain=mlp_gain, w_gate=w_gate, w_up=w_up, w_down=w_down, final_gain=final_gain, w_head=w_head)


epsilon = 1e-05
theta = 500000.0

def rms_scale(entries, scaling):
    entries = entries.astype(jnp.float32)
    inverse = lax.rsqrt(lax.optimization_barrier(jnp.mean(entries * entries, axis=-1, keepdims=True)) + epsilon)
    return entries * inverse * scaling.astype(jnp.float32)

def rotate(entries, positions):
    halfway = entries.shape[-1] // 2
    frequency = theta ** (-jnp.arange(halfway, dtype=jnp.float32) * 2.0 / entries.shape[-1])
    angles = positions.astype(jnp.float32)[:, None] * frequency[None, :]
    cosine = jnp.cos(angles)
    sine_part = jnp.sin(angles)
    former = entries[..., :halfway]
    latter = entries[..., halfway:]
    return jnp.concatenate([former * cosine - latter * sine_part, latter * cosine + former * sine_part], axis=-1)

def request_layout(length_row, slot_count):
    length_row = length_row.astype(jnp.int32)
    end_slot = jnp.cumsum(length_row, dtype=jnp.int32)
    start_slot = end_slot - length_row
    slot_ids = jnp.arange(slot_count, dtype=jnp.int32)
    member = (slot_ids[:, None] >= start_slot[None, :]) & (slot_ids[:, None] < end_slot[None, :])
    segment = lax.optimization_barrier(jnp.sum((slot_ids[:, None] >= end_slot[None, :]).astype(jnp.int32), axis=1))
    offset = lax.optimization_barrier(jnp.sum(jnp.where(member, start_slot[None, :], 0), axis=1)).astype(jnp.int32)
    return (member, segment, slot_ids - offset)

def allowed_pairs(segment):
    slot_ids = jnp.arange(segment.shape[0], dtype=jnp.int32)
    return (segment[:, None] == segment[None, :]) & (slot_ids[None, :] <= slot_ids[:, None])

def attend_heads(query, key_rows, value_rows, positions, allowed, repeat_times):
    slot_count = query.shape[0]
    query = rotate(query.reshape(slot_count, -1, HEAD_DIM).transpose(1, 0, 2), positions).astype(jnp.bfloat16)
    key_rows = rotate(key_rows.reshape(slot_count, -1, HEAD_DIM).transpose(1, 0, 2), positions).astype(jnp.bfloat16)
    value_rows = value_rows.reshape(slot_count, -1, HEAD_DIM).transpose(1, 0, 2).astype(jnp.bfloat16)
    key_rows = jnp.repeat(key_rows, repeat_times, axis=0)
    value_rows = jnp.repeat(value_rows, repeat_times, axis=0)
    scores = jnp.einsum('hqd,hkd->hqk', query.astype(jnp.float32), key_rows.astype(jnp.float32)) * HEAD_DIM ** (-0.5)
    scores = jnp.where(allowed[None], scores, -1e+30)
    highest = lax.optimization_barrier(jnp.max(scores, axis=-1, keepdims=True))
    weights = jnp.exp(scores - highest)
    probs = (weights / lax.optimization_barrier(jnp.sum(weights, axis=-1, keepdims=True))).astype(jnp.bfloat16)
    attended = jnp.einsum('hqk,hkd->hqd', probs.astype(jnp.float32), value_rows.astype(jnp.float32)).astype(jnp.bfloat16)
    return attended.transpose(1, 0, 2).reshape(slot_count, -1)

def reference(tokens, lengths, response, targets, attn_gain, w_query, w_key, w_value, output_weight, mlp_gain, w_gate, w_up, w_down, final_gain, w_head):
    finals = []
    members = []
    for tenant in range(TENANTS):
        tenant_rows = tokens[tenant * TOK_GRP:(tenant + 1) * TOK_GRP]
        member, segment, positions = request_layout(lengths[tenant], TOK_GRP)
        members.append(member.astype(jnp.float32))
        allowed = allowed_pairs(segment)
        per_model = []
        for model in range(2):
            normed = rms_scale(tenant_rows, attn_gain[model]).astype(jnp.bfloat16)
            query = jnp.dot(normed, w_query[model], preferred_element_type=jnp.float32)
            key_rows = jnp.dot(normed, w_key[model], preferred_element_type=jnp.float32)
            value_rows = jnp.dot(normed, w_value[model], preferred_element_type=jnp.float32)
            attended = attend_heads(query, key_rows, value_rows, positions, allowed, HEADS // KV_HEADS)
            residual = tenant_rows.astype(jnp.float32) + jnp.dot(attended, output_weight[model], preferred_element_type=jnp.float32)
            normed_mid = rms_scale(residual, mlp_gain[model]).astype(jnp.bfloat16)
            gate_part = jnp.dot(normed_mid, w_gate[model], preferred_element_type=jnp.float32)
            lift_part = jnp.dot(normed_mid, w_up[model], preferred_element_type=jnp.float32)
            hidden = (jax.nn.silu(gate_part) * lift_part).astype(jnp.bfloat16)
            final = residual + jnp.dot(hidden, w_down[model], preferred_element_type=jnp.float32)
            per_model.append(rms_scale(final, final_gain[model]).astype(jnp.bfloat16))
        finals.append(jnp.stack(per_model))
    finals = jnp.concatenate(finals, axis=1)
    block_rows = 32
    block_count = TOKENS // block_rows
    shaped = finals.reshape(2, block_count, block_rows, D).transpose(1, 0, 2, 3)
    wanted = targets.reshape(block_count, block_rows).astype(jnp.int32)

    def score_block(item):
        row_block, picks = item
        results = []
        for model in range(2):
            logits = jnp.dot(row_block[model], w_head[model], preferred_element_type=jnp.float32)
            highest = lax.optimization_barrier(jnp.max(logits, axis=-1, keepdims=True))
            normalizer = highest[:, 0] + jnp.log(lax.optimization_barrier(jnp.sum(jnp.exp(logits - highest), axis=-1)))
            chosen_token = jnp.take_along_axis(logits, picks[:, None], axis=1)[:, 0]
            results.append(chosen_token - normalizer)
        return jnp.stack(results)
    log_likelihood = lax.map(score_block, (shaped, wanted))
    log_likelihood = log_likelihood.transpose(1, 0, 2).reshape(2, TOKENS)
    token_diff = (log_likelihood[0] - log_likelihood[1]) * response.astype(jnp.float32)
    sums = []
    peaks = []
    for tenant in range(TENANTS):
        tenant_difference = token_diff[tenant * TOK_GRP:(tenant + 1) * TOK_GRP]
        sums.append(jnp.dot(tenant_difference, members[tenant], precision=lax.Precision.HIGHEST))
        peaks.append(lax.optimization_barrier(jnp.max(members[tenant] * jnp.abs(tenant_difference)[:, None], axis=0)))
    return (token_diff, jnp.stack(sums), jnp.stack(peaks))
```

```python
import jax
import jax.numpy as jnp
import ml_dtypes
import numpy as np
from jax import lax
from jax.experimental import pallas as pl
from jax.experimental.pallas import tpu as pltpu
from jax.sharding import PartitionSpec as P

D = 2048
HALF = 1024
HEAD_DIM = 64
TOK = 256
ROWS = 128
V_DEV = 1002
V_PAD = 1008
V_BLK = 336
CH = 1152
FF2 = 512
EPS = 1e-05
THETA = 500000.0
MESH = pl.DeviceIdType.MESH
F32 = jnp.float32
BF16 = jnp.bfloat16
NT = (((1,), (1,)), ((), ()))
ORDERS = ("yzx", "zxy", "xyz")


def rope_tables():
    frequency = (THETA ** (-np.arange(32, dtype=np.float32) * np.float32(2.0) / np.float32(64))).astype(np.float32)
    angles = (np.arange(128, dtype=np.float32)[:, None] * frequency[None, :]).astype(np.float32)
    cosine = np.cos(angles.astype(np.float64))
    sine = np.sin(angles.astype(np.float64))
    full = np.concatenate([np.tile(cosine, (1, 4)), np.tile(np.concatenate([-sine, sine], 1), (1, 2))], 1)
    full = full.astype(np.float32)
    pieces = []
    for _ in range(3):
        piece = full.astype(ml_dtypes.bfloat16)
        pieces.append(piece)
        full = full - piece.astype(np.float32)
    return np.stack(pieces)


def split3(values):
    first = values.astype(BF16).astype(F32)
    second = (values - first).astype(BF16).astype(F32)
    return first, second, values - first - second


def dot(a, b):
    return jnp.dot(a, b, preferred_element_type=F32)


def dot_nt(a, b):
    return lax.dot_general(a, b, NT, preferred_element_type=F32)


def kernel(
    pass_ref,
    len_ref,
    tok_hbm,
    resp_hbm,
    tgt_hbm,
    again_hbm,
    wq_hbm,
    wk_hbm,
    wv_hbm,
    ow_hbm,
    mgain_hbm,
    wg_hbm,
    wu_hbm,
    wd_hbm,
    fgain_hbm,
    wh_hbm,
    rope_hbm,
    tok_out,
    sum_out,
    peak_out,
    cnt_out,
    tok_v,
    resp_v,
    tgt_v,
    gain_v,
    wq_v,
    wkv_v,
    rope_v,
    o_v,
    wg_v,
    wu_v,
    wd_v,
    raw_v,
    head_v,
    x_v,
    att_s,
    att_r,
    part_v,
    part2_v,
    rs1_v,
    rs2_v,
    xa_v,
    g_v,
    st_v,
    sa_v,
    sb_v,
    sc_v,
    lsem,
    wss,
    wrs,
    ass,
    ars,
    r1s,
    r1r,
    a1s,
    a1r,
    r2s,
    r2r,
    gs,
    gr,
    ys,
    yr,
    bs,
    br,
    cs,
    cr,
):
    y = lax.axis_index("req")
    mp = lax.axis_index("mp")
    core = mp % 2
    chip = mp // 2
    z = chip // 4
    x = chip % 4
    other = 1 - core
    half = x % 2
    xh = x // 2
    group = z * 2 + xh

    def dev(yy, zz, xx, cc):
        return (yy, (zz * 4 + xx) * 2 + cc)

    sibling = dev(y, z, x, other)
    plane = [((z + i // 4) % 4, (x + i % 4) % 4) for i in range(1, 16)]
    column = [dev((y + i) % 4, z, x, core) for i in (1, 2, 3)]

    def remote(src, dst, send, recv, where):
        copy = pltpu.make_async_remote_copy(src, dst, send, recv, device_id=where, device_id_type=MESH)
        copy.start()
        return copy

    def local(src, dst, index):
        copy = pltpu.make_async_copy(src, dst, lsem.at[index])
        copy.start()
        return copy

    barrier = pltpu.get_barrier_semaphore()
    greeted = [sibling] + column + [dev(y, zz, xx, core) for zz, xx in plane]
    for where in greeted:
        pl.semaphore_signal(barrier, inc=1, device_id=where, device_id_type=MESH)

    kv_first = pl.multiple_of((mp // 8) * 128, 128)
    l_tok = local(tok_hbm, tok_v, 0)
    l_again = local(again_hbm, gain_v.at[0], 1)
    l_resp = local(resp_hbm, resp_v, 2)
    l_tgt = local(tgt_hbm, tgt_v, 3)
    l_rope = local(rope_hbm, rope_v, 4)
    l_wq = [local(wq_hbm.at[m], wq_v.at[pl.ds(64 * m, 64)], 5 + m) for m in range(2)]
    l_wk = local(wk_hbm.at[:, :, pl.ds(kv_first, 128)], wkv_v.at[:, :, pl.ds(0, 128)], 7)
    l_wv = local(wv_hbm.at[:, :, pl.ds(kv_first, 128)], wkv_v.at[:, :, pl.ds(128, 128)], 8)
    own_o = pl.multiple_of(core * 64, 64)
    own_f = pl.multiple_of(core * 256, 256)
    l_o = local(ow_hbm.at[core], o_v.at[pl.ds(own_o, 64)], 9)
    l_mgain = local(mgain_hbm, gain_v.at[1], 10)
    l_fgain = local(fgain_hbm, gain_v.at[2], 11)
    l_wg = local(wg_hbm.at[core], wg_v.at[:, pl.ds(own_f, 256)], 12)
    l_wu = local(wu_hbm.at[core], wu_v.at[:, pl.ds(own_f, 256)], 13)
    l_wd = local(wd_hbm.at[core], wd_v.at[pl.ds(own_f, 256)], 14)
    l_wh = local(wh_hbm, raw_v.at[pl.ds(0, V_DEV)], 15)

    ends = []
    total = jnp.int32(0)
    for j in range(8):
        total = total + len_ref[0, j]
        ends.append(total)
    lane_tok = lax.broadcasted_iota(jnp.int32, (1, TOK), 1)
    seg_row = jnp.zeros((1, TOK), jnp.int32)
    for j in range(8):
        seg_row = seg_row + (lane_tok >= ends[j]).astype(jnp.int32)
    sub_tok = lax.broadcasted_iota(jnp.int32, (TOK, 128), 0)
    start_tok = jnp.zeros((TOK, 128), jnp.int32)
    for j in range(7):
        start_tok = jnp.where(sub_tok >= ends[j], ends[j], start_tok)
    position = sub_tok - start_tok

    l_tok.wait()
    l_again.wait()

    @pl.loop(0, 8)
    def _(i):
        rows = pl.ds(pl.multiple_of(i * 32, 32), 32)
        block = tok_v[rows, :].astype(F32)
        inverse = lax.rsqrt(jnp.mean(block * block, axis=-1, keepdims=True) + EPS)
        block = block * inverse
        for m in range(2):
            x_v[m, rows, :] = (block * gain_v[0, m : m + 1, :]).astype(BF16)

    pl.semaphore_wait(barrier, len(greeted))
    w_o = remote(ow_hbm.at[other], o_v.at[pl.ds(own_o, 64)], wss.at[0], wrs.at[0], sibling)
    w_g = remote(wg_hbm.at[other], wg_v.at[:, pl.ds(own_f, 256)], wss.at[1], wrs.at[1], sibling)
    w_u = remote(wu_hbm.at[other], wu_v.at[:, pl.ds(own_f, 256)], wss.at[2], wrs.at[2], sibling)
    w_d = remote(wd_hbm.at[other], wd_v.at[pl.ds(own_f, 256)], wss.at[3], wrs.at[3], sibling)

    for copy in l_wq:
        copy.wait()
    l_wk.wait()
    l_wv.wait()
    l_rope.wait()
    l_resp.wait()
    l_tgt.wait()

    lane = lax.broadcasted_iota(jnp.int32, (TOK, 128), 1)
    pick = lane == position
    one_hot = jnp.where(pick, 1.0, 0.0).astype(BF16)
    turn = dot(one_hot, rope_v[0]) + dot(one_hot, rope_v[1]) + dot(one_hot, rope_v[2])
    cosine = turn[:, :128]
    sine = turn[:, 128:]

    low = lane < 64
    first_half = lane % 64 < 32

    def rotate(values):
        swapped = jnp.where(first_half, pltpu.roll(values, 96, 1), pltpu.roll(values, 32, 1))
        return (values * cosine + swapped * sine).astype(BF16)

    query = rotate(jnp.where(low, dot_nt(x_v[0], wq_v[...]), dot_nt(x_v[1], wq_v[...])))
    parity = (mp // 4) % 2
    kv = [dot(x_v[m], wkv_v[m]) for m in range(2)]

    def chosen(first, second):
        crossed = jnp.where(low, pltpu.roll(first, 64, 1), second)
        flipped = jnp.where(low, first, pltpu.roll(second, 64, 1))
        return jnp.where(parity == 0, flipped, crossed)

    key = rotate(chosen(kv[0][:, :128], kv[1][:, :128]))
    value = chosen(kv[0][:, 128:], kv[1][:, 128:]).astype(BF16)

    resp = jnp.where(resp_v[...] > 0, 1.0, 0.0).astype(BF16)
    upper = (
        lax.broadcasted_iota(jnp.int32, (TOK, TOK), 0) <= lax.broadcasted_iota(jnp.int32, (TOK, TOK), 1)
    )
    ranks = dot(jnp.broadcast_to(resp, (16, TOK)), jnp.where(upper, 1.0, 0.0).astype(BF16))[0:1]
    count = jnp.max(ranks, axis=1, keepdims=True)
    ranks = ranks.astype(jnp.int32) - 1 - ROWS * pass_ref[0]
    ranks = jnp.where(resp_v[...] > 0, ranks, -1)
    sub_rank = lax.broadcasted_iota(jnp.int32, (ROWS, TOK), 0)
    chosen_rows = sub_rank == ranks
    select = jnp.where(chosen_rows, 1.0, 0.0)
    select_bf = select.astype(BF16)
    slots = jnp.sum(jnp.where(chosen_rows, lane_tok, 0), axis=1, keepdims=True)
    segments = jnp.sum(jnp.where(chosen_rows, seg_row, 0), axis=1, keepdims=True)
    allowed = (segments == seg_row) & (lane_tok <= slots)

    q_rows = dot(select_bf, query).astype(BF16)
    attended = []
    for m in range(2):
        key_m = jnp.where(low == (m == 0), key, jnp.zeros_like(key))
        scores = dot_nt(q_rows, key_m) * HEAD_DIM ** (-0.5)
        scores = jnp.where(allowed, scores, -1e30)
        weights = jnp.exp(scores - jnp.max(scores, axis=1, keepdims=True))
        probs = (weights / jnp.sum(weights, axis=1, keepdims=True)).astype(BF16)
        attended.append(dot(probs, value))
    lane_r = lax.broadcasted_iota(jnp.int32, (ROWS, 128), 1)
    att = jnp.where(lane_r < 64, attended[0], attended[1])
    att_s[...] = pltpu.roll(att, 64, 1).astype(BF16)
    a_x = remote(att_s, att_r, ass, ars, sibling)
    mine = lane_r // 64 == core
    own_tok = dot(
        jnp.where(
            lax.broadcasted_iota(jnp.int32, (16, TOK), 0) + group * 16 == ranks, 1.0, 0.0
        ).astype(BF16),
        tok_v[:, pl.ds(pl.multiple_of(half * HALF, HALF), HALF)],
    )
    targets = tgt_v[pl.ds(y, 1), :]
    own_target = jnp.sum(
        jnp.where(
            lax.broadcasted_iota(jnp.int32, (16, TOK), 0) + group * 16 == ranks,
            jnp.broadcast_to(targets, (16, TOK)),
            0,
        ),
        axis=1,
        keepdims=True,
    )
    l_o.wait()
    l_mgain.wait()
    l_fgain.wait()
    a_x.wait()
    w_o.wait()
    joined = jnp.where(mine, att.astype(BF16), att_r[...])

    def scatter(product, part, recv, ssem, rsem):
        for hh in range(2):
            part[hh] = product(hh).astype(BF16).reshape(4, 2, 16, HALF)
        copies = []
        for i, (zz, xx) in enumerate(plane):
            copies.append(
                remote(
                    part.at[xx % 2, zz, xx // 2], recv.at[i], ssem.at[i], rsem.at[i], dev(y, zz, xx, core)
                )
            )
        return copies

    def collect(copies, part, recv):
        acc = part[half, z, xh].astype(F32)
        for i, copy in enumerate(copies):
            copy.wait()
            acc = acc + recv[i].astype(F32)
        return acc

    lane_s = lax.broadcasted_iota(jnp.int32, (16, 128), 1)

    def packed(rows, which):
        gain = gain_v[which, pl.ds(core, 1), pl.ds(pl.multiple_of(half * HALF, HALF), HALF)]
        squares = jnp.sum(rows * rows, axis=1, keepdims=True)
        stats = jnp.zeros((16, 128), F32)
        for i, piece in enumerate(split3(squares)):
            stats = jnp.where(lane_s == i, piece, stats)
        for i, shift in enumerate((16, 8, 0)):
            digit = ((own_target >> shift) & 255).astype(F32)
            stats = jnp.where((lane_s == 3 + i) & (half == 0), digit, stats)
        return (rows * gain).astype(BF16), stats.astype(BF16)

    r1 = scatter(
        lambda hh: dot(joined, o_v[:, hh * HALF : (hh + 1) * HALF]), part_v, rs1_v, r1s, r1r
    )

    l_wh.wait()
    raw_v[V_DEV:V_PAD] = jnp.zeros((V_PAD - V_DEV, 2, D), BF16)

    @pl.loop(0, V_PAD // 16)
    def _(i):
        rows = pl.ds(pl.multiple_of(i * 16, 16), 16)
        head_v[0:2, rows, :] = jnp.swapaxes(raw_v[rows], 0, 1)

    w_h = remote(head_v.at[other], head_v.at[2], wss.at[4], wrs.at[4], sibling)

    residual = own_tok + collect(r1, part_v, rs1_v)
    body, stats = packed(residual, 1)
    xa_v[half, z, xh, :, 0:HALF] = body
    xa_v[half, z, xh, :, HALF:CH] = stats
    a1 = [
        remote(xa_v.at[half, z, xh], xa_v.at[half, z, xh], a1s.at[i], a1r.at[i], dev(y, zz, xx, core))
        for i, (zz, xx) in enumerate(plane)
    ]
    l_wg.wait()
    l_wu.wait()
    l_wd.wait()
    w_g.wait()
    w_u.wait()
    w_d.wait()
    for copy in a1:
        copy.wait()
    rows_a = [xa_v[hh, :, :, :, 0:HALF].reshape(ROWS, HALF) for hh in range(2)]
    sq = xa_v[0, :, :, :, HALF:CH].reshape(ROWS, 128).astype(F32)
    sq = sq + xa_v[1, :, :, :, HALF:CH].reshape(ROWS, 128).astype(F32)
    sq = jnp.sum(jnp.where(lane_r < 3, sq, 0.0), axis=1, keepdims=True)
    inverse = lax.rsqrt(sq / D + EPS)
    gate = (dot(rows_a[0], wg_v[0:HALF]) + dot(rows_a[1], wg_v[HALF:D])) * inverse
    lift = (dot(rows_a[0], wu_v[0:HALF]) + dot(rows_a[1], wu_v[HALF:D])) * inverse
    hidden = ((gate / (1.0 + jnp.exp(-gate))) * lift).astype(BF16)
    r2 = scatter(
        lambda hh: dot(hidden, wd_v[:, hh * HALF : (hh + 1) * HALF]), part2_v, rs2_v, r2s, r2r
    )
    final = residual + collect(r2, part2_v, rs2_v)
    body, stats = packed(final, 2)
    g_v[half, y, z, xh, :, 0:HALF] = body
    g_v[half, y, z, xh, :, HALF:CH] = stats

    every = slice(None)
    for stage in range(3):
        copies = []
        for step in (1, 3, 2):
            for part, order in enumerate(ORDERS):
                at = {"y": y, "z": z, "x": x}
                done = order[:stage]
                h_at = every if "x" in done else half
                x_at = every if "x" in done else xh
                y_at = every if "y" in done else y
                z_at = every if "z" in done else z
                view = g_v.at[h_at, y_at, z_at, x_at, :, pl.ds(384 * part, 384)]
                axis = order[stage]
                at[axis] = (at[axis] + step) % 4
                copies.append(
                    remote(
                        view,
                        view,
                        gs.at[stage, part, step - 1],
                        gr.at[stage, part, step - 1],
                        dev(at["y"], at["z"], at["x"], core),
                    )
                )
        for copy in copies:
            copy.wait()

    inv_rows, tgt_rows = [], []
    for t in range(4):
        st = g_v[0, t, :, :, :, HALF:CH].reshape(ROWS, 128).astype(F32)
        st = (st + g_v[1, t, :, :, :, HALF:CH].reshape(ROWS, 128).astype(F32)).T
        inv_rows.append(lax.rsqrt((st[0:1] + st[1:2] + st[2:3]) / D + EPS))
        tgt_rows.append((st[3:4] * 65536.0 + st[4:5] * 256.0 + st[5:6]).astype(jnp.int32))
    inv_row = jnp.concatenate(inv_rows, axis=1)
    tgt_row = jnp.concatenate(tgt_rows, axis=1)
    n_rows = 4 * ROWS
    keys_h = [g_v[hh, :, :, :, :, 0:HALF].reshape(n_rows, HALF) for hh in range(2)]
    state = (jnp.full((1, n_rows), -1e30, F32), jnp.zeros((1, n_rows), F32), jnp.zeros((1, n_rows), F32))
    for which in range(2):
        if which:
            w_h.wait()
        slot = core if which == 0 else 2
        owner = core if which == 0 else other
        wanted = tgt_row - (y * 32 + chip * 2 + owner) * V_DEV

        def block(i, carry, slot=slot, wanted=wanted):
            peak, norm, hit = carry
            first = pl.multiple_of(i * V_BLK, 16)
            left = head_v[slot, pl.ds(first, V_BLK), 0:HALF]
            right = head_v[slot, pl.ds(first, V_BLK), HALF:D]
            logits = (dot_nt(left, keys_h[0]) + dot_nt(right, keys_h[1])) * inv_row
            ids = lax.broadcasted_iota(jnp.int32, (V_BLK, n_rows), 0) + first
            inside = ids < V_DEV
            logits = jnp.where(inside, logits, -1e30)
            top = jnp.maximum(peak, jnp.max(logits, axis=0, keepdims=True))
            norm = norm * jnp.exp(peak - top) + jnp.sum(jnp.exp(logits - top), axis=0, keepdims=True)
            hit = hit + jnp.sum(jnp.where((ids == wanted) & inside, logits, 0.0), axis=0, keepdims=True)
            return top, norm, hit

        state = lax.fori_loop(0, V_PAD // V_BLK, block, state)
    peak, norm, hit = state
    lse = peak + jnp.log(norm)

    sub8 = lax.broadcasted_iota(jnp.int32, (8, 128), 0)
    for t in range(4):
        cut = slice(t * ROWS, (t + 1) * ROWS)
        tile = jnp.where(sub8 == 0, lse[:, cut], jnp.where(sub8 == 1, hit[:, cut], count))
        st_v[t] = tile
    copies = []
    for i, where in enumerate(column):
        copies.append(remote(st_v.at[(y + i + 1) % 4], sa_v.at[i], ys.at[i], yr.at[i], where))
    for copy in copies:
        copy.wait()

    def merge(tiles):
        top = tiles[0]
        for tile in tiles[1:]:
            top = jnp.maximum(top, tile)
        spread = jnp.zeros_like(top)
        added = jnp.zeros_like(top)
        for tile in tiles:
            spread = spread + jnp.exp(tile - top)
            added = added + tile
        return top, top + jnp.log(spread), added

    top, lse_t, hits = merge([st_v[y]] + [sa_v[i] for i in range(3)])
    cnt_out[...] = top[2:3].astype(jnp.int32)
    sb_v[0] = jnp.where(sub8 == 0, lse_t, hits)
    copies = []
    for i, (zz, xx) in enumerate(plane):
        copies.append(remote(sb_v.at[0], sb_v.at[i + 1], bs.at[i], br.at[i], dev(y, zz, xx, core)))
    for copy in copies:
        copy.wait()
    top, lse_t, hits = merge([sb_v[i] for i in range(16)])
    sc_v[0] = jnp.broadcast_to(hits[1:2] - lse_t[0:1], (8, 128))
    last = remote(sc_v.at[0], sc_v.at[1], cs, cr, sibling)
    last.wait()
    sign = (1 - 2 * core).astype(F32)
    gap = (sc_v[0] - sc_v[1]) * sign
    sub16 = lax.broadcasted_iota(jnp.int32, (16, 128), 0)
    gap_pieces = jnp.zeros((16, 128), F32)
    for i, piece in enumerate(split3(gap[0:1])):
        gap_pieces = jnp.where(sub16 == i, piece, gap_pieces)
    spread_gap = dot(gap_pieces.astype(BF16), select_bf)
    diff = spread_gap[0:1] + spread_gap[1:2] + spread_gap[2:3]

    eye = lax.broadcasted_iota(jnp.int32, (8, 8), 0) == lax.broadcasted_iota(jnp.int32, (8, 8), 1)
    sub_t = lax.broadcasted_iota(jnp.int32, (8, TOK), 0)
    lane_t = lax.broadcasted_iota(jnp.int32, (8, TOK), 1)

    def to_row(col):
        return jnp.sum(jnp.where(eye, col, 0.0), axis=0, keepdims=True)

    member = sub_t == seg_row
    spread_diff = jnp.broadcast_to(diff, (8, TOK))
    tok_out[...] = to_row(jnp.sum(jnp.where(lane_t == sub_t + mp * 8, spread_diff, 0.0), axis=1, keepdims=True))
    sum_out[...] = to_row(jnp.sum(jnp.where(member, spread_diff, 0.0), axis=1, keepdims=True))
    peak_out[...] = to_row(jnp.max(jnp.where(member, jnp.abs(spread_diff), 0.0), axis=1, keepdims=True))


def run_pass(number, tokens, lengths, response, targets, attn_gain, w_query, w_key, w_value, output_weight, mlp_gain, w_gate, w_up, w_down, final_gain, w_head, rope):
    smem = pl.BlockSpec(memory_space=pltpu.SMEM)
    anyp = pl.BlockSpec(memory_space=pl.ANY)
    vmem = pl.BlockSpec(memory_space=pltpu.VMEM)
    dma = pltpu.SemaphoreType.DMA
    return pl.pallas_call(
        kernel,
        name="score_pass",
        out_shape=(
            jax.ShapeDtypeStruct((1, 8), F32),
            jax.ShapeDtypeStruct((1, 8), F32),
            jax.ShapeDtypeStruct((1, 8), F32),
            jax.ShapeDtypeStruct((1, 128), jnp.int32),
        ),
        in_specs=[smem, smem] + [anyp] * 15,
        out_specs=(vmem,) * 4,
        scratch_shapes=[
            pltpu.VMEM((TOK, D), BF16),
            pltpu.VMEM((1, TOK), jnp.int32),
            pltpu.VMEM((4, TOK), jnp.int32),
            pltpu.VMEM((3, 2, D), F32),
            pltpu.VMEM((128, D), BF16),
            pltpu.VMEM((2, D, 256), BF16),
            pltpu.VMEM((3, 128, 256), BF16),
            pltpu.VMEM((128, D), BF16),
            pltpu.VMEM((D, FF2), BF16),
            pltpu.VMEM((D, FF2), BF16),
            pltpu.VMEM((FF2, D), BF16),
            pltpu.VMEM((V_PAD, 2, D), BF16),
            pltpu.VMEM((3, V_PAD, D), BF16),
            pltpu.VMEM((2, TOK, D), BF16),
            pltpu.VMEM((ROWS, 128), BF16),
            pltpu.VMEM((ROWS, 128), BF16),
            pltpu.VMEM((2, 4, 2, 16, HALF), BF16),
            pltpu.VMEM((2, 4, 2, 16, HALF), BF16),
            pltpu.VMEM((15, 16, HALF), BF16),
            pltpu.VMEM((15, 16, HALF), BF16),
            pltpu.VMEM((2, 4, 2, 16, CH), BF16),
            pltpu.VMEM((2, 4, 4, 2, 16, CH), BF16),
            pltpu.VMEM((4, 8, 128), F32),
            pltpu.VMEM((3, 8, 128), F32),
            pltpu.VMEM((16, 8, 128), F32),
            pltpu.VMEM((2, 8, 128), F32),
            dma((16,)),
            dma((5,)),
            dma((5,)),
            dma,
            dma,
            dma((15,)),
            dma((15,)),
            dma((15,)),
            dma((15,)),
            dma((15,)),
            dma((15,)),
            dma((3, 3, 3)),
            dma((3, 3, 3)),
            dma((3,)),
            dma((3,)),
            dma((15,)),
            dma((15,)),
            dma,
            dma,
        ],
        compiler_params=pltpu.CompilerParams(
            collective_id=1, has_side_effects=True, vmem_limit_bytes=56 * 2**20
        ),
    )(
        number,
        lengths,
        tokens,
        response,
        targets,
        attn_gain,
        w_query,
        w_key,
        w_value,
        output_weight,
        mlp_gain,
        w_gate,
        w_up,
        w_down,
        final_gain,
        w_head,
        rope,
    )


def per_device(tokens, lengths, response, targets, attn_gain, w_query, w_key, w_value, output_weight, mlp_gain, w_gate, w_up, w_down, final_gain, w_head):
    operands = (
        tokens,
        lengths,
        response.reshape(1, TOK),
        targets.reshape(4, TOK),
        attn_gain,
        jnp.swapaxes(w_query, 1, 2),
        w_key,
        w_value,
        output_weight,
        mlp_gain,
        w_gate,
        w_up,
        w_down,
        final_gain,
        jnp.transpose(w_head, (2, 0, 1)),
        jnp.asarray(rope_tables()),
    )
    token_out, sums, peaks, count = run_pass(jnp.zeros((1,), jnp.int32), *operands)

    def again(first):
        more = run_pass(jnp.ones((1,), jnp.int32), *operands)
        return first[0] + more[0], first[1] + more[1], jnp.maximum(first[2], more[2])

    token_out, sums, peaks = lax.cond(
        count[0, 0] > ROWS, again, lambda first: first, (token_out, sums, peaks)
    )
    return token_out.reshape(8), sums, peaks


def solution(mesh):
    placed = (
        P("req", None),
        P("req", None),
        P("req"),
        P(),
        P(),
        P(None, None, "mp"),
        P(),
        P(),
        P(None, "mp", None),
        P(),
        P(None, None, "mp"),
        P(None, None, "mp"),
        P(None, "mp", None),
        P(),
        P(None, None, ("req", "mp")),
    )
    return jax.shard_map(
        per_device,
        mesh=mesh,
        in_specs=placed,
        out_specs=(P(("req", "mp")), P("req", None), P("req", None)),
        check_vma=False,
    )
```
